32 devices in a mesh: group: 2 (over x), adapter: 16 (over z, y, core).
Axes of the slice: x: 2, y: 2, z: 4, core: 2. Of those that a mesh axis runs over, the one named last changes fastest.
Arguments:
- tokens: bfloat16 [1024, 8192], P(('group', 'adapter')), parts along dimension 0, may hold values from -6 to 6
- kept_weight_entries: bfloat16 [4096, 28672], P(None, 'adapter'), may hold values from -0.09375 to 0.09375
- kept_row_pattern: int32 [2048, 28672], P(None, 'adapter'), may hold values from 0 to 5
- request_adapter: int32 [1024, 1], P('group'), parts along dimension 0, may hold values from 0 to 15; in each aligned block of 32 rows (0 to 31, 32 to 63, ...) at most 4 rows name the same one
- adapter_storage_slot: int32 [16], replicated, may hold values from 0 to 15, each once
- adapter_down_maps: bfloat16 [16, 8192, 64], P('adapter'), may hold values from -0.0625 to 0.0625
- adapter_up_maps: bfloat16 [16, 64, 28672], P(None, None, 'adapter'), may hold values from -0.75 to 0.75
Outputs:
- projected: bfloat16 [1024, 28672], P('group', 'adapter'), parts along dimension 0
The draws below stay inside these ranges and needn't reach their ends.
There are 2 independent parts, one for each index of `group`. The reference program is written for one: setup_inputs(seed, part) draws one part's arguments, and reference() takes and returns one part's arrays. A program takes and returns all parts, laid end to end along the dimension named above; an argument that names none is the same for every part. Nothing has to cross between parts.
Inputs may be any that keep to these rules, and one draw needn't show every extreme that they name: `request_adapter`: in each aligned block of 32 requests no adapter is named by more than 4 requests, a bound that some block reaches. `adapter_storage_slot`: each slot holds one adapter. `kept_row_pattern`: codes of the kept pair as in the reference program.
All inputs are finite; a program needn't handle non-finite values.
Results may differ from the reference program's by a relative error of at most 0.0046.
Values may be sent and summed in bfloat16 or wider, within the bound.
A program may use at most 320 MiB of HBM per device.

```python
import math
import jax
import jax.numpy as jnp
import numpy as np
from jax import lax

MODEL_WIDTH = 8192
HIDDEN_UNITS = 28672
ADAPTER_RANK = 64
R_DEV = 32
ROWS = 512
ADAPTER_COUNT = 16
CAP = 4


def touch_ends(entries, own_key, low, top_value):
    longest = entries.shape.index(max(entries.shape))
    spots = []
    for shift in (0, 1):
        where = [jax.random.randint(jax.random.fold_in(own_key, axis), (), 0, length) for axis, length in enumerate(entries.shape)]
        where[longest] = (where[longest] + shift) % entries.shape[longest]
        spots.append(tuple(where))
    return entries.at[spots[0]].set(low).at[spots[1]].set(top_value)


def steps_of(key, extent, cuts, least, largest):
    level = 1.0
    for position, shards_of in cuts:
        draws = jax.random.uniform(jax.random.fold_in(jax.random.fold_in(key, 6), position), (shards_of,), jnp.float32, least / len(cuts), largest / len(cuts))
        level = level * jnp.repeat(jnp.exp(draws), extent[position] // shards_of).reshape((-1,) + (1,) * (len(extent) - 1 - position))
    return level


def shared_out(key, own, number, rows, amount, top, bound, slope):
    sequence = jax.random.permutation(key, amount)
    packed, ordinary = portions_of(amount, rows * top, bound, slope, True), portions_of(amount, rows * top, bound, slope, False)
    places = jnp.arange(amount)

    def named(tallies, offset_by):
        used = int((tallies > 0).sum())
        fixed = max(1, used // 4)
        moved = fixed + (places - fixed + offset_by * (used - fixed)) % max(1, amount - fixed)
        return jnp.zeros((amount,), jnp.int32).at[sequence[jnp.where(places < fixed, places, moved)]].set(jnp.asarray(tallies, jnp.int32))

    tallies = jnp.where(number % 4 == 0, named(packed, number // 4), named(ordinary, number - number // 4 - 1))
    mixed = jax.random.permutation(jax.random.fold_in(own, 3), amount)
    donor, taker = mixed[0:amount // 2 * 2:2], mixed[1:amount // 2 * 2:2]
    slack = jnp.minimum(tallies[donor] - 1, bound - tallies[taker]) // 2
    slack = jnp.where((donor == sequence[0]) | (taker == sequence[0]) | (tallies[taker] == 0), 0, jnp.maximum(slack, 0))
    moved = jax.random.randint(jax.random.fold_in(own, 4), (amount // 2,), 0, 1 << 20) % (slack + 1)
    tallies = tallies.at[donor].add(-moved).at[taker].add(moved)
    items = jnp.searchsorted(jnp.cumsum(tallies), jnp.arange(rows * top), side="right").astype(jnp.int32)
    table = items.reshape(top, rows).T
    table = table[jax.random.permutation(jax.random.fold_in(own, 1), rows)]
    offset_by = jax.random.randint(jax.random.fold_in(own, 2), (rows, 1), 0, top)
    return jnp.take_along_axis(table, (jnp.arange(top)[None, :] + offset_by) % top, axis=1)


def portions_of(number_of, total, limit, slope, full):
    portions = [(1 << 20) // math.isqrt(rank ** slope) + 1 for rank in range(1, number_of + 1)]
    largest = limit if full else min(limit, max(-(-total // number_of), total * portions[0] // sum(portions)))
    least = 1 if total - largest >= number_of - 1 else 0
    holding, spare = [largest] + [least] * (number_of - 1), total - largest - least * (number_of - 1)
    while spare > 0:
        free = [i for i in range(1, number_of) if holding[i] < largest] or [i for i in range(1, number_of) if holding[i] < limit]
        mass, budget = sum([portions[i] for i in free]), spare
        for i in free:
            addition = min(limit - holding[i], max(1, budget * portions[i] // mass), spare)
            holding[i] = holding[i] + addition
            spare = spare - addition
    return np.array(holding)


def bell_draw(stream_key, shape, scale, bound, cuts=(), held_as=jnp.bfloat16):
    entries = jax.random.normal(stream_key, shape, jnp.float32) * scale
    if len(cuts) > 0:
        entries = steps_of(stream_key, shape, cuts, -0.22, 0.18) * entries
    return jnp.clip(entries, min=-bound, max=bound).astype(held_as)


def setup_inputs(seed: int = 0, part: int = 0) -> dict:
    splits = jax.random.split(jax.random.key(seed), 8)
    own_keys = jax.random.split(jax.random.fold_in(splits[7], part), 8)
    tokens = bell_draw(own_keys[0], (ROWS, MODEL_WIDTH), 1.0, 6.0, ((0, 16),))
    kept_weight_entries = bell_draw(splits[1], (MODEL_WIDTH // 2, HIDDEN_UNITS), (MODEL_WIDTH // 2) ** -0.5, 0.09375, ((1, 16),))
    kept_row_pattern = touch_ends(jax.random.randint(splits[2], (MODEL_WIDTH // 4, HIDDEN_UNITS), 0, 6), jax.random.fold_in(splits[2], 1), 0, 5).astype(jnp.int32)
    request_adapter_keys = jax.random.split(jax.random.fold_in(own_keys[3], 1), ROWS // R_DEV)
    request_adapter_turns = jax.random.permutation(jax.random.fold_in(own_keys[3], 3), ROWS // R_DEV)
    request_adapter = jax.vmap(lambda own, number: shared_out(jax.random.fold_in(own_keys[3], 2), own, number, R_DEV, ADAPTER_COUNT, 1, CAP, 2))(request_adapter_keys, request_adapter_turns).reshape((ROWS, 1))
    adapter_storage_slot = jax.random.permutation(splits[4], ADAPTER_COUNT).astype(jnp.int32)
    adapter_down_maps = bell_draw(splits[5], (ADAPTER_COUNT, MODEL_WIDTH, ADAPTER_RANK), MODEL_WIDTH ** -0.5, 0.0625, ((0, 16),))
    adapter_up_maps = bell_draw(splits[6], (ADAPTER_COUNT, ADAPTER_RANK, HIDDEN_UNITS), ADAPTER_RANK ** -0.5, 0.75, ((2, 16),))
    return dict(tokens=tokens, kept_weight_entries=kept_weight_entries, kept_row_pattern=kept_row_pattern, request_adapter=request_adapter, adapter_storage_slot=adapter_storage_slot, adapter_down_maps=adapter_down_maps, adapter_up_maps=adapter_up_maps)


ADAPTER_SCALE = 2.0


def expand_sparse(values, pattern):
    quarter = pattern.shape[0]
    width = pattern.shape[1]
    first = (pattern >= 3).astype(jnp.int32) + (pattern >= 5).astype(jnp.int32)
    second = 1 + (pattern == 1).astype(jnp.int32) + 2 * (pattern == 2).astype(jnp.int32) + (pattern == 3).astype(jnp.int32) + 2 * (pattern == 4).astype(jnp.int32) + 2 * (pattern == 5).astype(jnp.int32)
    pairs = values.reshape(quarter, 2, width)
    value_one = pairs[:, 0, :]
    value_two = pairs[:, 1, :]
    zeros_row = jnp.zeros_like(value_one)
    placed = [jnp.where(first == place, value_one, zeros_row) + jnp.where(second == place, value_two, zeros_row) for place in range(4)]
    return jnp.stack(placed, axis=1).reshape(quarter * 4, width)


def reference(tokens, kept_weight_entries, kept_row_pattern, request_adapter, adapter_storage_slot, adapter_down_maps, adapter_up_maps):
    block = math.gcd(HIDDEN_UNITS, 1024)
    count = HIDDEN_UNITS // block

    def one_block(index):
        start = (index * block).astype(jnp.int32)
        values = lax.dynamic_slice_in_dim(kept_weight_entries, start, block, 1)
        pattern = lax.dynamic_slice_in_dim(kept_row_pattern, start, block, 1)
        dense = expand_sparse(values, pattern)
        return jnp.dot(tokens, dense, preferred_element_type=jnp.float32)

    parts_out = lax.map(one_block, jnp.arange(count, dtype=jnp.int32))
    sparse_output = jnp.transpose(parts_out, (1, 0, 2)).reshape(tokens.shape[0], HIDDEN_UNITS)
    table = (request_adapter[:, 0:1] == jnp.arange(ADAPTER_COUNT, dtype=jnp.int32)[None, :]).astype(jnp.int32)
    row_slot = jnp.sum(table * adapter_storage_slot[None, :], axis=1).astype(jnp.int32)
    onehot = (row_slot[:, None] == jnp.arange(ADAPTER_COUNT, dtype=jnp.int32)[None, :]).astype(jnp.float32)
    all_low_rank = jnp.einsum("qw,gwt->qgt", tokens.astype(jnp.float32), adapter_down_maps.astype(jnp.float32))
    low = jnp.sum(all_low_rank * onehot[:, :, None], axis=1).astype(jnp.bfloat16)
    dense_weight = (onehot.astype(jnp.bfloat16)[:, :, None] * low[:, None, :]).reshape(tokens.shape[0], ADAPTER_COUNT * ADAPTER_RANK)
    low_rank_update = jnp.dot(dense_weight, adapter_up_maps.reshape(ADAPTER_COUNT * ADAPTER_RANK, HIDDEN_UNITS), preferred_element_type=jnp.float32)
    return (sparse_output + ADAPTER_SCALE * low_rank_update).astype(jnp.bfloat16)
```

```python
import functools

import jax
import jax.numpy as jnp
from jax import lax
from jax.experimental import pallas as pl
from jax.experimental.pallas import tpu as pltpu
from jax.sharding import PartitionSpec as P

ADAPTER_SCALE = 2.0
WAVES = 4
GROUPS = 128
MESH = pl.DeviceIdType.MESH
LEFT, RIGHT, ACROSS, TWIN = range(4)


def kernel(
    holders, across, capacity, slot_ref, tokens_ref, request_ref, values_hbm, pattern_hbm, down_hbm, up_hbm,
    out_ref, x, dense, total, vbuf, pbuf, down, down_p, up, low, low_all, spread, key,
    send_sem, recv_sem, low_send, low_recv, vsem, psem, misc_sem,
):
    rows_dev, width = tokens_ref.shape
    rows = rows_dev * holders
    hidden = up.shape[1]
    per_holder = holders * capacity
    line = holders // (2 * across)
    depth = 4 * GROUPS
    steps = width // depth
    wave_width = width // WAVES
    per_wave = wave_width // depth
    ticks = WAVES * line
    ratio = ticks // steps
    tn = 256 if hidden % 256 == 0 else 128
    me = lax.axis_index("adapter")
    core = lax.rem(me, 2)
    ypos = lax.rem(lax.div(me, 2), across)
    zpos = lax.div(me, 2 * across)

    def holder(z, y, c):
        return (z * across + y) * 2 + c

    def fetch(step):
        slot = lax.rem(step, 2)
        return (
            pltpu.make_async_copy(
                values_hbm.at[pl.ds(pl.multiple_of(step * 2 * GROUPS, 2 * GROUPS), 2 * GROUPS)],
                vbuf.at[slot], vsem.at[slot]),
            pltpu.make_async_copy(
                pattern_hbm.at[pl.ds(pl.multiple_of(step * GROUPS, GROUPS), GROUPS)],
                pbuf.at[slot], psem.at[slot]),
        )

    down_copy = pltpu.make_async_copy(down_hbm, down, misc_sem.at[0])
    up_copy = pltpu.make_async_copy(up_hbm, up, misc_sem.at[1])

    barrier = pltpu.get_barrier_semaphore()

    @pl.loop(1, holders)
    def _(i):
        pl.semaphore_signal(
            barrier, inc=1, device_id={"adapter": lax.rem(me + i, holders)}, device_id_type=MESH)

    for c in fetch(0):
        c.start()
    down_copy.start()
    up_copy.start()

    a = lax.broadcasted_iota(jnp.int32, (depth, depth), 0)
    b = lax.broadcasted_iota(jnp.int32, (depth, depth), 1)
    order = (a == 4 * (b & (GROUPS - 1)) + b // GROUPS).astype(jnp.float32).astype(jnp.bfloat16)
    order_t = (b == 4 * (a & (GROUPS - 1)) + a // GROUPS).astype(jnp.float32).astype(jnp.bfloat16)
    own_rows = pl.ds(pl.multiple_of(me * rows_dev, rows_dev), rows_dev)
    for s in range(steps):
        piece = jnp.dot(
            tokens_ref[:, s * depth:(s + 1) * depth], order, preferred_element_type=jnp.float32)
        x[s // per_wave, own_rows, (s % per_wave) * depth:(s % per_wave + 1) * depth] = piece.astype(
            jnp.bfloat16)

    pl.semaphore_wait(barrier, holders - 1)

    def copy(wave, owner, way):
        target = (
            holder(zpos - 1, ypos, core), holder(zpos + 1, ypos, core),
            holder(zpos, across - 1 - ypos, core), holder(zpos, ypos, 1 - core))[way]
        target = lax.rem(target + holders, holders)
        chunk = x.at[wave, pl.ds(pl.multiple_of(owner * rows_dev, rows_dev), rows_dev)]
        return pltpu.make_async_remote_copy(
            src_ref=chunk, dst_ref=chunk, send_sem=send_sem.at[wave, owner, way],
            recv_sem=recv_sem.at[wave, owner], device_id={"adapter": target}, device_id_type=MESH)

    def arrived(wave, owner):
        copy(wave, owner, TWIN).wait_recv()

    def ways_of_own(wave, do):
        @pl.when(zpos > 0)
        def _():
            do(copy(wave, me, LEFT))

        @pl.when(zpos < line - 1)
        def _():
            do(copy(wave, me, RIGHT))

        if across > 1:
            do(copy(wave, me, ACROSS))
        do(copy(wave, me, TWIN))

    def forwards(wave, hop, do, wait):
        @pl.when((hop < line - 1) & (zpos - 1 - hop >= 0))
        def _():
            owner = holder(zpos - 1 - hop, ypos, core)
            if wait:
                arrived(wave, owner)

            @pl.when(zpos < line - 1)
            def _():
                do(copy(wave, owner, RIGHT))

            if across > 1:
                do(copy(wave, owner, ACROSS))
            do(copy(wave, owner, TWIN))

        @pl.when((hop < line - 1) & (zpos + 1 + hop <= line - 1))
        def _():
            owner = holder(zpos + 1 + hop, ypos, core)
            if wait:
                arrived(wave, owner)

            @pl.when(zpos > 0)
            def _():
                do(copy(wave, owner, LEFT))

            if across > 1:
                do(copy(wave, owner, ACROSS))
            do(copy(wave, owner, TWIN))

    def from_across(wave, level, do, wait):
        if across == 1:
            return

        @pl.when(zpos - level >= 0)
        def _():
            owner = holder(zpos - level, across - 1 - ypos, core)
            if wait:
                arrived(wave, owner)
            do(copy(wave, owner, TWIN))

        @pl.when((level > 0) & (zpos + level <= line - 1))
        def _():
            owner = holder(zpos + level, across - 1 - ypos, core)
            if wait:
                arrived(wave, owner)
            do(copy(wave, owner, TWIN))

    start = lambda c: c.start()
    sent = lambda c: c.wait_send()

    ways_of_own(0, start)

    request = request_ref[...]
    slot = jnp.zeros(request.shape, jnp.int32)
    for i in range(holders):
        slot = jnp.where(request == i, slot_ref[i], slot)
    slot_f = slot.astype(jnp.float32)
    wide = jnp.broadcast_to(slot_f, (rows, 128))
    slot_row = jnp.transpose(wide)[0:1, :]
    ra = lax.broadcasted_iota(jnp.int32, (rows, rows), 0)
    rb = lax.broadcasted_iota(jnp.int32, (rows, rows), 1)
    before = (slot_f == slot_row) & (ra // rows_dev == rb // rows_dev) & (rb < ra)
    place = jnp.sum(before.astype(jnp.float32), axis=1, keepdims=True)
    block = (lax.broadcasted_iota(jnp.int32, (rows, 1), 0) // rows_dev).astype(jnp.float32)
    key[...] = jnp.broadcast_to(slot_f * per_holder + block * capacity + place, (rows, 128))

    total[...] = jnp.zeros_like(total)
    low[...] = jnp.zeros_like(low)
    down_copy.wait()

    qa = lax.broadcasted_iota(jnp.int32, (2 * GROUPS, 2 * GROUPS), 0)
    qb = lax.broadcasted_iota(jnp.int32, (2 * GROUPS, 2 * GROUPS), 1)
    pairs = (qb == 2 * (8 * (qa // 16) + (qa & 7)) + ((qa // 8) & 1)).astype(jnp.float32).astype(
        jnp.bfloat16)

    def expand(step):
        @pl.when(step + 1 < steps)
        def _():
            for c in fetch(step + 1):
                c.start()

        for c in fetch(step):
            c.wait()
        slot = lax.rem(step, 2)
        base = step * depth
        for j in range(hidden // tn):
            cols = pl.ds(j * tn, tn)
            both = jnp.dot(pairs, vbuf[slot, :, cols], preferred_element_type=jnp.float32)
            both = both.reshape(GROUPS // 8, 2, 8, tn)
            one = both[:, 0].reshape(GROUPS, tn)
            two = both[:, 1].reshape(GROUPS, tn)
            p = pbuf[slot, :, cols]
            zero = jnp.zeros_like(one)
            planes = (
                jnp.where(p < 3, one, zero),
                jnp.where(p == 0, two, jnp.where((p == 3) | (p == 4), one, zero)),
                jnp.where(p == 5, one, jnp.where((p == 1) | (p == 3), two, zero)),
                jnp.where((p == 2) | (p >= 4), two, zero),
            )
            for k, plane in enumerate(planes):
                dense[pl.ds(pl.multiple_of(base + k * GROUPS, GROUPS), GROUPS), cols] = plane.astype(
                    jnp.bfloat16)
        here = pl.ds(pl.multiple_of(base, depth), depth)
        part = jnp.dot(order_t, down[here, :], preferred_element_type=jnp.float32).astype(jnp.bfloat16)
        down_p[here, :] = jnp.concatenate([part, part], axis=1)

    def all_here(wave):
        @pl.loop(0, holders // 2)
        def _(i):
            arrived(wave, 2 * i + 1 - core)

    def low_of(wave):
        here = pl.ds(pl.multiple_of(wave * wave_width, wave_width), wave_width)
        low[...] += jnp.dot(x[wave], down_p[here, :], preferred_element_type=jnp.float32)

    def multiply(wave):
        here = pl.ds(pl.multiple_of(wave * wave_width, wave_width), wave_width)

        @pl.loop(0, hidden // tn)
        def _(j):
            cols = pl.ds(pl.multiple_of(j * tn, tn), tn)
            total[:, cols] += jnp.dot(
                x[wave], dense[here, cols], preferred_element_type=jnp.float32)

    @pl.loop(0, ticks)
    def _(t):
        wave, hop = lax.div(t, line), lax.rem(t, line)

        @pl.when(lax.rem(t, ratio) == 0)
        def _():
            expand(lax.div(t, ratio))

        @pl.when((hop == 0) & (wave + 1 < WAVES))
        def _():
            ways_of_own(wave + 1, start)

        forwards(wave, hop, start, True)

        @pl.when(t > 0)
        def _():
            from_across(lax.div(t - 1, line), lax.rem(t - 1, line), start, True)

        @pl.when((hop == 1) & (wave > 0))
        def _():
            all_here(wave - 1)
            low_of(wave - 1)
            multiply(wave - 1)

    from_across(WAVES - 1, line - 1, start, True)
    all_here(WAVES - 1)
    low_of(WAVES - 1)

    key_row = jnp.transpose(key[...])[0:1, :]
    mine = lax.broadcasted_iota(jnp.int32, (per_holder, rows), 0) + me * per_holder
    pick = (mine.astype(jnp.float32) == key_row).astype(jnp.float32).astype(jnp.bfloat16)
    low_all[me] = jnp.dot(
        pick, low[...].astype(jnp.bfloat16), preferred_element_type=jnp.float32).astype(jnp.bfloat16)

    def low_copy(owner, target):
        return pltpu.make_async_remote_copy(
            src_ref=low_all.at[owner], dst_ref=low_all.at[owner], send_sem=low_send.at[target],
            recv_sem=low_recv.at[owner], device_id={"adapter": target}, device_id_type=MESH)

    @pl.loop(1, holders)
    def _(i):
        low_copy(me, lax.rem(me + i, holders)).start()

    multiply(WAVES - 1)
    up_copy.wait()

    @pl.loop(1, holders)
    def _(i):
        low_copy(lax.rem(me + i, holders), lax.rem(me + i, holders)).wait_recv()

    tall = low_all[...].reshape(holders * per_holder, 128)
    names = lax.broadcasted_iota(jnp.int32, (rows, holders * per_holder), 1).astype(jnp.float32)
    choose = (names == key[:, 0:1]).astype(jnp.float32).astype(jnp.bfloat16)
    rows_low = ADAPTER_SCALE * jnp.dot(choose, tall, preferred_element_type=jnp.float32)
    rank = up.shape[0] // holders
    first = key[...]
    lane = lax.broadcasted_iota(jnp.int32, (rows, 128), 1) // rank
    for j in range(up.shape[0] // 128):
        least = ((lane + (128 // rank) * j) * per_holder).astype(jnp.float32)
        held = (first >= least) & (first < least + per_holder)
        spread[:, j * 128:(j + 1) * 128] = jnp.where(held, rows_low, 0.0).astype(jnp.bfloat16)

    @pl.loop(0, hidden // tn)
    def _(j):
        cols = pl.ds(pl.multiple_of(j * tn, tn), tn)
        out_ref[:, cols] = (
            total[:, cols] + jnp.dot(spread[...], up[:, cols], preferred_element_type=jnp.float32)
        ).astype(jnp.bfloat16)

    @pl.loop(1, holders)
    def _(i):
        low_copy(me, lax.rem(me + i, holders)).wait_send()

    @pl.loop(0, WAVES)
    def _(wave):
        ways_of_own(wave, sent)

    @pl.loop(0, ticks)
    def _(t):
        wave, hop = lax.div(t, line), lax.rem(t, line)
        forwards(wave, hop, sent, False)
        from_across(wave, hop, sent, False)


def body(tokens, values, pattern, request, slots, down, up):
    holders = lax.axis_size("adapter")
    rows_dev, width = tokens.shape
    rows = rows_dev * holders
    adapters, rank, hidden = up.shape
    across = 2 if holders == 16 else 1
    capacity = max(2, 2 * rows_dev // holders)
    bf16, f32 = jnp.bfloat16, jnp.float32
    anywhere = pl.BlockSpec(memory_space=pl.ANY)
    vmem = pl.BlockSpec(memory_space=pltpu.VMEM)
    dma = pltpu.SemaphoreType.DMA
    return pl.pallas_call(
        functools.partial(kernel, holders, across, capacity),
        out_shape=jax.ShapeDtypeStruct((rows, hidden), bf16),
        in_specs=[pl.BlockSpec(memory_space=pltpu.SMEM), vmem, vmem] + [anywhere] * 4,
        out_specs=vmem,
        scratch_shapes=[
            pltpu.VMEM((WAVES, rows, width // WAVES), bf16),
            pltpu.VMEM((width, hidden), bf16),
            pltpu.VMEM((rows, hidden), f32),
            pltpu.VMEM((2, 2 * GROUPS, hidden), bf16),
            pltpu.VMEM((2, GROUPS, hidden), jnp.int32),
            pltpu.VMEM((width, rank), bf16),
            pltpu.VMEM((width, 2 * rank), bf16),
            pltpu.VMEM((adapters * rank, hidden), bf16),
            pltpu.VMEM((rows, 2 * rank), f32),
            pltpu.VMEM((holders, holders * capacity, 2 * rank), bf16),
            pltpu.VMEM((rows, adapters * rank), bf16),
            pltpu.VMEM((rows, 128), f32),
            dma((WAVES, holders, 4)),
            dma((WAVES, holders)),
            dma((holders,)),
            dma((holders,)),
            dma((2,)),
            dma((2,)),
            dma((2,)),
        ],
        compiler_params=pltpu.CompilerParams(
            collective_id=0, has_side_effects=True, vmem_limit_bytes=62 * 1024 * 1024),
        cost_estimate=pl.CostEstimate(
            flops=2 * rows * width * hidden, bytes_accessed=40 * 1024 * 1024, transcendentals=0),
    )(slots, tokens, request, values, pattern, down.reshape(width, rank), up.reshape(adapters * rank, hidden))


def solution(mesh):
    placed = (
        P(("group", "adapter"), None),
        P(None, "adapter"),
        P(None, "adapter"),
        P("group", None),
        P(),
        P("adapter", None, None),
        P(None, None, "adapter"),
    )
    return jax.shard_map(
        body, mesh=mesh, in_specs=placed, out_specs=P("group", "adapter"), check_vma=False
    )
```

```python
import functools

import jax
import jax.numpy as jnp
from jax import lax
from jax.experimental import pallas as pl
from jax.experimental.pallas import tpu as pltpu
from jax.sharding import PartitionSpec as P

ADAPTER_SCALE = 2.0
WAVES = 2
CHUNK = 256
GROUPS = 128
MESH = pl.DeviceIdType.MESH
LEFT, RIGHT, ACROSS, TWIN = range(4)


def kernel(
    holders, across, capacity, slot_ref, tokens_ref, request_ref, values_hbm, pattern_hbm, down_hbm, up_hbm,
    out_ref, x, dense, total, vbuf, pbuf, down, down_p, up, low, low_all, spread, key,
    send_sem, recv_sem, low_send, low_recv, vsem, psem, misc_sem,
):
    rows_dev, width = tokens_ref.shape
    rows = rows_dev * holders
    hidden = up.shape[1]
    per_holder = holders * capacity
    line = holders // (2 * across)
    depth = 4 * GROUPS
    steps = width // depth
    wave_width = width // WAVES
    per_wave = wave_width // depth
    ticks = WAVES * line
    ratio = max(1, ticks // steps)
    per_tick = max(1, steps // ticks)
    tn = 256 if hidden % 256 == 0 else 128
    me = lax.axis_index("adapter")
    core = lax.rem(me, 2)
    ypos = lax.rem(lax.div(me, 2), across)
    zpos = lax.div(me, 2 * across)

    def holder(z, y, c):
        return (z * across + y) * 2 + c

    def fetch(step):
        slot = lax.rem(step, 2)
        return (
            pltpu.make_async_copy(
                values_hbm.at[pl.ds(pl.multiple_of(step * 2 * GROUPS, 2 * GROUPS), 2 * GROUPS)],
                vbuf.at[slot], vsem.at[slot]),
            pltpu.make_async_copy(
                pattern_hbm.at[pl.ds(pl.multiple_of(step * GROUPS, GROUPS), GROUPS)],
                pbuf.at[slot], psem.at[slot]),
        )

    down_copy = pltpu.make_async_copy(down_hbm, down, misc_sem.at[0])
    up_copy = pltpu.make_async_copy(up_hbm, up, misc_sem.at[1])

    barrier = pltpu.get_barrier_semaphore()

    @pl.loop(1, holders)
    def _(i):
        pl.semaphore_signal(
            barrier, inc=1, device_id={"adapter": lax.rem(me + i, holders)}, device_id_type=MESH)

    for c in fetch(0):
        c.start()
    down_copy.start()
    up_copy.start()

    a = lax.broadcasted_iota(jnp.int32, (CHUNK, CHUNK), 0)
    b = lax.broadcasted_iota(jnp.int32, (CHUNK, CHUNK), 1)
    order = (a == 4 * (b & (CHUNK // 4 - 1)) + b // (CHUNK // 4)).astype(jnp.float32).astype(jnp.bfloat16)
    own_rows = pl.ds(pl.multiple_of(me * rows_dev, rows_dev), rows_dev)
    chunks = wave_width // CHUNK

    def reorder(source, wave):
        high = source.shape[0]
        pieces = [source[:, (wave * chunks + i) * CHUNK:(wave * chunks + i + 1) * CHUNK] for i in range(chunks)]
        moved = jnp.dot(
            jnp.concatenate(pieces, axis=0), order, preferred_element_type=jnp.float32).astype(jnp.bfloat16)
        return [moved[i * high:(i + 1) * high] for i in range(chunks)]

    def reorder_tokens(wave):
        for i, piece in enumerate(reorder(tokens_ref, wave)):
            x[wave, own_rows, i * CHUNK:(i + 1) * CHUNK] = piece

    reorder_tokens(0)

    pl.semaphore_wait(barrier, holders - 1)

    def copy(wave, owner, way):
        target = (
            holder(zpos - 1, ypos, core), holder(zpos + 1, ypos, core),
            holder(zpos, across - 1 - ypos, core), holder(zpos, ypos, 1 - core))[way]
        target = lax.rem(target + holders, holders)
        chunk = x.at[wave, pl.ds(pl.multiple_of(owner * rows_dev, rows_dev), rows_dev)]
        return pltpu.make_async_remote_copy(
            src_ref=chunk, dst_ref=chunk, send_sem=send_sem.at[wave, owner, way],
            recv_sem=recv_sem.at[wave, owner], device_id={"adapter": target}, device_id_type=MESH)

    def arrived(wave, owner):
        copy(wave, owner, TWIN).wait_recv()

    def ways_of_own(wave, do):
        @pl.when(zpos > 0)
        def _():
            do(copy(wave, me, LEFT))

        @pl.when(zpos < line - 1)
        def _():
            do(copy(wave, me, RIGHT))

        if across > 1:
            do(copy(wave, me, ACROSS))
        do(copy(wave, me, TWIN))

    def forwards(wave, hop, do, wait):
        @pl.when((hop < line - 1) & (zpos - 1 - hop >= 0))
        def _():
            owner = holder(zpos - 1 - hop, ypos, core)
            if wait:
                arrived(wave, owner)

            @pl.when(zpos < line - 1)
            def _():
                do(copy(wave, owner, RIGHT))

            if across > 1:
                do(copy(wave, owner, ACROSS))
            do(copy(wave, owner, TWIN))

        @pl.when((hop < line - 1) & (zpos + 1 + hop <= line - 1))
        def _():
            owner = holder(zpos + 1 + hop, ypos, core)
            if wait:
                arrived(wave, owner)

            @pl.when(zpos > 0)
            def _():
                do(copy(wave, owner, LEFT))

            if across > 1:
                do(copy(wave, owner, ACROSS))
            do(copy(wave, owner, TWIN))

    def from_across(wave, level, do, wait):
        if across == 1:
            return

        @pl.when(zpos - level >= 0)
        def _():
            owner = holder(zpos - level, across - 1 - ypos, core)
            if wait:
                arrived(wave, owner)
            do(copy(wave, owner, TWIN))

        @pl.when((level > 0) & (zpos + level <= line - 1))
        def _():
            owner = holder(zpos + level, across - 1 - ypos, core)
            if wait:
                arrived(wave, owner)
            do(copy(wave, owner, TWIN))

    start = lambda c: c.start()
    sent = lambda c: c.wait_send()

    ways_of_own(0, start)
    for wave in range(1, WAVES):
        reorder_tokens(wave)

    request = request_ref[...]
    slot = jnp.zeros(request.shape, jnp.int32)
    for i in range(holders):
        slot = jnp.where(request == i, slot_ref[i], slot)
    slot_row = slot.astype(jnp.float32)
    slot_f = jnp.transpose(jnp.broadcast_to(slot_row, (128, rows)))[:, 0:1]
    ra = lax.broadcasted_iota(jnp.int32, (rows, rows), 0)
    rb = lax.broadcasted_iota(jnp.int32, (rows, rows), 1)
    before = (slot_f == slot_row) & (ra // rows_dev == rb // rows_dev) & (rb < ra)
    place = jnp.sum(before.astype(jnp.float32), axis=1, keepdims=True)
    block = (lax.broadcasted_iota(jnp.int32, (rows, 1), 0) // rows_dev).astype(jnp.float32)
    key[...] = jnp.broadcast_to(slot_f * per_holder + block * capacity + place, (rows, 128))

    total[...] = jnp.zeros_like(total)
    low[...] = jnp.zeros_like(low)
    down_copy.wait()
    for wave in range(WAVES):
        for i, piece in enumerate(reorder(down, wave)):
            down_p[wave, :, i * CHUNK:(i + 1) * CHUNK] = jnp.concatenate([piece, piece], axis=0)

    qa = lax.broadcasted_iota(jnp.int32, (2 * GROUPS, 2 * GROUPS), 0)
    qb = lax.broadcasted_iota(jnp.int32, (2 * GROUPS, 2 * GROUPS), 1)
    pairs = (qb == 2 * (8 * (qa // 16) + (qa & 7)) + ((qa // 8) & 1)).astype(jnp.float32).astype(
        jnp.bfloat16)

    def expand(step):
        @pl.when(step + 1 < steps)
        def _():
            for c in fetch(step + 1):
                c.start()

        for c in fetch(step):
            c.wait()
        slot = lax.rem(step, 2)
        base = step * depth
        for j in range(hidden // tn):
            cols = pl.ds(j * tn, tn)
            both = jnp.dot(pairs, vbuf[slot, :, cols], preferred_element_type=jnp.float32)
            both = both.reshape(GROUPS // 8, 2, 8, tn)
            one = both[:, 0].reshape(GROUPS, tn).astype(jnp.bfloat16)
            two = both[:, 1].reshape(GROUPS, tn).astype(jnp.bfloat16)
            p = pbuf[slot, :, cols].astype(jnp.float32).astype(jnp.bfloat16)
            zero = jnp.zeros_like(one)
            planes = (
                jnp.where(p < 3, one, zero),
                jnp.where(p == 0, two, jnp.where((p == 3) | (p == 4), one, zero)),
                jnp.where(p == 5, one, jnp.where((p == 1) | (p == 3), two, zero)),
                jnp.where((p == 2) | (p >= 4), two, zero),
            )
            quarter = CHUNK // 4
            for k, plane in enumerate(planes):
                for u in range(GROUPS // quarter):
                    place = pl.multiple_of(base + u * CHUNK + k * quarter, quarter)
                    dense[pl.ds(place, quarter), cols] = plane[u * quarter:(u + 1) * quarter]

    def all_here(wave):
        @pl.loop(0, holders // 2)
        def _(i):
            arrived(wave, 2 * i + 1 - core)

    def low_of(wave):
        low[...] += lax.dot_general(
            x[wave], down_p[wave], (((1,), (1,)), ((), ())), preferred_element_type=jnp.float32)

    def multiply(wave, least, most):
        here = pl.ds(pl.multiple_of(wave * wave_width, wave_width), wave_width)

        @pl.loop(least, most)
        def _(j):
            cols = pl.ds(pl.multiple_of(j * tn, tn), tn)
            total[:, cols] += jnp.dot(
                x[wave], dense[here, cols], preferred_element_type=jnp.float32)

    @pl.loop(0, ticks)
    def _(t):
        wave, hop = lax.div(t, line), lax.rem(t, line)

        @pl.when(lax.rem(t, ratio) == 0)
        def _():
            @pl.loop(0, per_tick)
            def _(i):
                expand(lax.div(t, ratio) * per_tick + i)

        @pl.when((hop == 0) & (wave + 1 < WAVES))
        def _():
            ways_of_own(wave + 1, start)

        forwards(wave, hop, start, True)

        @pl.when(t > 0)
        def _():
            from_across(lax.div(t - 1, line), lax.rem(t - 1, line), start, True)

        @pl.when((hop == 1) & (wave > 0))
        def _():
            all_here(wave - 1)
            low_of(wave - 1)

        @pl.when((hop > 0) & (wave > 0))
        def _():
            tiles = hidden // tn
            multiply(wave - 1, lax.div(tiles * (hop - 1), line - 1), lax.div(tiles * hop, line - 1))

    from_across(WAVES - 1, line - 1, start, True)
    all_here(WAVES - 1)
    low_of(WAVES - 1)

    key_row = jnp.transpose(key[...])[0:1, :]
    mine = lax.broadcasted_iota(jnp.int32, (per_holder, rows), 0) + me * per_holder
    pick = (mine.astype(jnp.float32) == key_row).astype(jnp.float32).astype(jnp.bfloat16)
    low_all[me] = jnp.dot(
        pick, low[...].astype(jnp.bfloat16), preferred_element_type=jnp.float32).astype(jnp.bfloat16)

    def low_copy(owner, target):
        return pltpu.make_async_remote_copy(
            src_ref=low_all.at[owner], dst_ref=low_all.at[owner], send_sem=low_send.at[target],
            recv_sem=low_recv.at[owner], device_id={"adapter": target}, device_id_type=MESH)

    @pl.loop(1, holders)
    def _(i):
        low_copy(me, lax.rem(me + i, holders)).start()

    multiply(WAVES - 1, 0, hidden // tn)
    up_copy.wait()

    @pl.loop(1, holders)
    def _(i):
        low_copy(lax.rem(me + i, holders), lax.rem(me + i, holders)).wait_recv()

    tall = low_all[...].reshape(holders * per_holder, 128)
    names = lax.broadcasted_iota(jnp.int32, (rows, holders * per_holder), 1).astype(jnp.float32)
    choose = (names == key[:, 0:1]).astype(jnp.float32).astype(jnp.bfloat16)
    rows_low = ADAPTER_SCALE * jnp.dot(choose, tall, preferred_element_type=jnp.float32)
    rank = up.shape[0] // holders
    first = key[...]
    lane = lax.broadcasted_iota(jnp.int32, (rows, 128), 1) // rank
    for j in range(up.shape[0] // 128):
        least = ((lane + (128 // rank) * j) * per_holder).astype(jnp.float32)
        held = (first >= least) & (first < least + per_holder)
        spread[:, j * 128:(j + 1) * 128] = jnp.where(held, rows_low, 0.0).astype(jnp.bfloat16)

    @pl.loop(0, hidden // tn)
    def _(j):
        cols = pl.ds(pl.multiple_of(j * tn, tn), tn)
        out_ref[:, cols] = (
            total[:, cols] + jnp.dot(spread[...], up[:, cols], preferred_element_type=jnp.float32)
        ).astype(jnp.bfloat16)

    @pl.loop(1, holders)
    def _(i):
        low_copy(me, lax.rem(me + i, holders)).wait_send()

    @pl.loop(0, WAVES)
    def _(wave):
        ways_of_own(wave, sent)

    @pl.loop(0, ticks)
    def _(t):
        wave, hop = lax.div(t, line), lax.rem(t, line)
        forwards(wave, hop, sent, False)
        from_across(wave, hop, sent, False)


def body(tokens, values, pattern, request, slots, down, up):
    holders = lax.axis_size("adapter")
    rows_dev, width = tokens.shape
    rows = rows_dev * holders
    adapters, rank, hidden = up.shape
    across = 2 if holders == 16 else 1
    capacity = max(2, 2 * rows_dev // holders)
    bf16, f32 = jnp.bfloat16, jnp.float32
    anywhere = pl.BlockSpec(memory_space=pl.ANY)
    vmem = pl.BlockSpec(memory_space=pltpu.VMEM)
    dma = pltpu.SemaphoreType.DMA
    return pl.pallas_call(
        functools.partial(kernel, holders, across, capacity),
        out_shape=jax.ShapeDtypeStruct((rows, hidden), bf16),
        in_specs=[pl.BlockSpec(memory_space=pltpu.SMEM), vmem, vmem] + [anywhere] * 4,
        out_specs=vmem,
        scratch_shapes=[
            pltpu.VMEM((WAVES, rows, width // WAVES), bf16),
            pltpu.VMEM((width, hidden), bf16),
            pltpu.VMEM((rows, hidden), f32),
            pltpu.VMEM((2, 2 * GROUPS, hidden), bf16),
            pltpu.VMEM((2, GROUPS, hidden), jnp.int32),
            pltpu.VMEM((rank, width), bf16),
            pltpu.VMEM((WAVES, 2 * rank, width // WAVES), bf16),
            pltpu.VMEM((adapters * rank, hidden), bf16),
            pltpu.VMEM((rows, 2 * rank), f32),
            pltpu.VMEM((holders, holders * capacity, 2 * rank), bf16),
            pltpu.VMEM((rows, adapters * rank), bf16),
            pltpu.VMEM((rows, 128), f32),
            dma((WAVES, holders, 4)),
            dma((WAVES, holders)),
            dma((holders,)),
            dma((holders,)),
            dma((2,)),
            dma((2,)),
            dma((2,)),
        ],
        compiler_params=pltpu.CompilerParams(
            collective_id=0, has_side_effects=True, vmem_limit_bytes=62 * 1024 * 1024),
        cost_estimate=pl.CostEstimate(
            flops=2 * rows * width * hidden, bytes_accessed=40 * 1024 * 1024, transcendentals=0),
    )(slots, tokens, request.reshape(1, rows), values, pattern, down[0].T, up.reshape(adapters * rank, hidden))


def solution(mesh):
    placed = (
        P(("group", "adapter"), None),
        P(None, "adapter"),
        P(None, "adapter"),
        P("group", None),
        P(),
        P("adapter", None, None),
        P(None, None, "adapter"),
    )
    return jax.shard_map(
        body, mesh=mesh, in_specs=placed, out_specs=P("group", "adapter"), check_vma=False
    )
```
